32 devices in a mesh: grp: 2 (over x), attn: 1, exp: 16 (over z, y, core).
Axes of the slice: x: 2, y: 2, z: 4, core: 2. Of those that a mesh axis runs over, the one named last changes fastest.
Arguments:
- hidden_rows: bfloat16 [16, 64, 5120], P('exp', 'grp', 'attn'), may hold values from -6 to 6
- routes: int32 [16, 64, 6], P('exp'), may hold values from 0 to 15, all different within a row; in each aligned block of 64 rows (0 to 63, 64 to 127, ..., all dimensions but the last counted through in order) at most 32 rows name the same one
- route_gain: float32 [16, 64, 6], P('exp'), may hold values from 0.1 to 1
- gate_weight: bfloat16 [16, 1536, 5120], P('exp', 'grp', 'attn'), may hold values from -0.078125 to 0.078125
- up_weight: bfloat16 [16, 1536, 5120], P('exp', 'grp', 'attn'), may hold values from -0.078125 to 0.078125
- down_weight: bfloat16 [16, 1536, 5120], P('exp', 'grp', 'attn'), may hold values from -0.21875 to 0.21875
Outputs:
- layer_out: bfloat16 [16, 64, 5120], P('exp', 'grp', 'attn')
The draws below stay inside these ranges and needn't reach their ends.
Inputs may be any that keep to these rules, and one draw needn't show every extreme that they name: `routes`: each row names 6 different experts. Among the 64 rows of one line no expert is named more than 32 times, and in every draw some expert is named exactly 32 times by the rows of one line; every expert is named somewhere.
All inputs are finite; a program needn't handle non-finite values.
Results may differ from the reference program's by a relative error of at most 0.022.
Values may be sent and summed in bfloat16 or wider, within the bound.
No kernel may reach another device: no remote copies, remote signals or barrier semaphores. Data moves between devices by JAX's collectives and lax.ppermute only.
A program may use at most 128 MiB of HBM per device.

```python
import math
import jax
import jax.numpy as jnp
import numpy as np
from jax import lax

D = 5120
FF = 1536
TOPK = 6
SLAB_ROWS = 64
LINES = 16
EXPERTS = 16
CAPS = 32
N_GRP = 2


def spiked(array, stream_key, source, target, shards_of, factor):
    owner, partner = [(jnp.arange(array.shape[axis_at]) // (array.shape[axis_at] // shards_of)).reshape([-1 if axis == axis_at else 1 for axis in range(array.ndim)]) for axis_at in (source, target)]
    chosen = jax.random.permutation(stream_key, shards_of)[partner]
    strong = (owner == chosen) | (owner == (partner + shards_of // 2) % shards_of)
    return jnp.where(strong, factor * array, array)


def levels(key, shape, pieces, low, high):
    factor_of, own = 1.0, jax.random.fold_in(key, 6)
    for axis_at, blocks in pieces:
        steps = jnp.exp(jax.random.uniform(jax.random.fold_in(own, axis_at), (blocks,), jnp.float32, low / len(pieces), high / len(pieces)))
        factor_of = factor_of * jnp.repeat(steps, shape[axis_at] // blocks).reshape([-1 if axis == axis_at else 1 for axis in range(len(shape))])
    return factor_of


def routed_block(key, own, number, rows, amount, top, reach, lean):
    order = jax.random.permutation(key, amount)
    crowded, ordinary = load_shares(amount, rows * top, reach, lean, True), load_shares(amount, rows * top, reach, lean, False)
    places = jnp.arange(amount)

    def named(tallies, rotation):
        used = int((tallies > 0).sum())
        fixed = max(1, used // 4)
        moved = fixed + (places - fixed + rotation * (used - fixed)) % max(1, amount - fixed)
        return jnp.zeros((amount,), jnp.int32).at[order[jnp.where(places < fixed, places, moved)]].set(jnp.asarray(tallies, jnp.int32))

    tallies = jnp.where(number % 4 == 0, named(crowded, number // 4), named(ordinary, number - number // 4 - 1))
    mixed = jax.random.permutation(jax.random.fold_in(own, 3), amount)
    donor, sink = mixed[0:amount // 2 * 2:2], mixed[1:amount // 2 * 2:2]
    slack = jnp.minimum(tallies[donor] - 1, reach - tallies[sink]) // 2
    slack = jnp.where((donor == order[0]) | (sink == order[0]) | (tallies[sink] == 0), 0, jnp.maximum(slack, 0))
    moved = jax.random.randint(jax.random.fold_in(own, 4), (amount // 2,), 0, 1 << 20) % (slack + 1)
    tallies = tallies.at[donor].add(-moved).at[sink].add(moved)
    members = jnp.searchsorted(jnp.cumsum(tallies), jnp.arange(rows * top), side="right").astype(jnp.int32)
    table = members.reshape(top, rows).T
    table = table[jax.random.permutation(jax.random.fold_in(own, 1), rows)]
    rotation = jax.random.randint(jax.random.fold_in(own, 2), (rows, 1), 0, top)
    return jnp.take_along_axis(table, (jnp.arange(top)[None, :] + rotation) % top, axis=1)


def load_shares(count, total, most, lean, full):
    portions = [(1 << 20) // math.isqrt(standing ** lean) + 1 for standing in range(1, count + 1)]
    largest = most if full else min(most, max(-(-total // count), total * portions[0] // sum(portions)))
    least = 1 if total - largest >= count - 1 else 0
    holding, surplus = [largest] + [least] * (count - 1), total - largest - least * (count - 1)
    while surplus > 0:
        candidates = [i for i in range(1, count) if holding[i] < largest] or [i for i in range(1, count) if holding[i] < most]
        pool, left = sum([portions[i] for i in candidates]), surplus
        for i in candidates:
            more = min(most - holding[i], max(1, left * portions[i] // pool), surplus)
            holding[i] = holding[i] + more
            surplus = surplus - more
    return np.array(holding)


def centred(stream_key, extent, deviation, limit, split=(), held_as=jnp.bfloat16):
    gain = levels(stream_key, extent, split, -0.22, 0.18) if split else 1.0
    array = jax.random.normal(stream_key, extent, jnp.float32) * deviation * gain
    return jnp.minimum(jnp.maximum(array, -limit), limit).astype(held_as)


def heavy_noise(own_key, shape, scale, reach, pieces, heavy, held_as=jnp.bfloat16):
    entries = scale * jax.random.normal(own_key, shape, jnp.float32)
    if pieces:
        entries = entries * levels(own_key, shape, pieces, -0.22, 0.18)
    return jnp.clip(spiked(entries, jax.random.fold_in(own_key, 3), *heavy), -reach, reach).astype(held_as)


def setup_inputs(seed: int = 0) -> dict:
    seeds = jax.random.split(jax.random.key(seed), 7)
    hidden_rows = centred(seeds[0], (LINES, SLAB_ROWS, D), 1.0, 6.0, ((0, 16), (1, 2)))
    routes_keys = jax.random.split(jax.random.fold_in(seeds[1], 1), LINES * SLAB_ROWS // SLAB_ROWS)
    routes_turns = jax.random.permutation(jax.random.fold_in(seeds[1], 3), LINES * SLAB_ROWS // SLAB_ROWS)
    routes = jax.vmap(lambda own, number: routed_block(jax.random.fold_in(seeds[1], 2), own, number, SLAB_ROWS, EXPERTS, TOPK, CAPS, 2))(routes_keys, routes_turns).reshape((LINES, SLAB_ROWS, TOPK))
    route_gain = jnp.clip(jnp.exp(math.log(1.0) - 2.3025851 * jax.random.uniform(seeds[2], (LINES, SLAB_ROWS, TOPK), jnp.float32) ** levels(seeds[2], (LINES, SLAB_ROWS, TOPK), ((0, 16),), -0.2, 0.2)), 0.1, 1.0)
    gate_weight = centred(seeds[3], (EXPERTS, FF, D), D ** -0.5, 0.078125, ((0, 16), (1, 2)))
    up_weight = centred(seeds[4], (EXPERTS, FF, D), D ** -0.5, 0.078125, ((0, 16), (1, 2)))
    down_weight = heavy_noise(seeds[5], (EXPERTS, FF, D), FF ** -0.5, 0.21875, ((0, 16), (1, 2)), (1, 2, 2, 2.0))
    return dict(hidden_rows=hidden_rows, routes=routes, route_gain=route_gain, gate_weight=gate_weight, up_weight=up_weight, down_weight=down_weight)


def slot_tables(routes_line):
    slab = routes_line.shape[0]
    picks = (routes_line[:, :, None] == jnp.arange(EXPERTS, dtype=jnp.int32)[None, None, :]).astype(jnp.float32)
    counts = jnp.sum(picks, axis=1)
    lower = (jnp.arange(slab)[:, None] > jnp.arange(slab)[None, :]).astype(jnp.float32)
    before = jnp.dot(lower, counts, precision=lax.Precision.HIGHEST)
    grid = jnp.arange(CAPS).astype(jnp.float32)
    send = counts[:, :, None] * (before[:, :, None] == grid).astype(jnp.float32)
    send = jnp.transpose(send, (1, 2, 0))
    gather_tab = picks[:, :, :, None] * (before[:, None, :, None] == grid).astype(jnp.float32)
    return send, gather_tab.reshape(slab, picks.shape[1], EXPERTS * CAPS)


def reference(hidden_rows, routes, route_gain, gate_weight, up_weight, down_weight):
    sends, gathers = jax.vmap(slot_tables)(routes)
    rows_f = hidden_rows.astype(jnp.float32)
    block = FF // N_GRP
    dims = (((1,), (1,)), ((), ()))

    def one_expert(items):
        index, w_gate, w_up, w_down = items
        select = lax.dynamic_index_in_dim(sends, index, 1, keepdims=False)
        taken = jnp.einsum("lcs,lsd->lcd", select, rows_f).astype(jnp.bfloat16)
        flat = taken.reshape(-1, D)
        gate = lax.dot_general(flat, w_gate, dims, preferred_element_type=jnp.float32)
        upper = lax.dot_general(flat, w_up, dims, preferred_element_type=jnp.float32)
        act = (jax.nn.silu(gate) * upper).astype(jnp.bfloat16)
        act_b = act.astype(jnp.float32).reshape(-1, N_GRP, block)
        down_b = w_down.astype(jnp.float32).reshape(N_GRP, block, D)
        parts = jnp.einsum("mab,abd->mad", act_b, down_b).astype(jnp.bfloat16)
        parts = lax.optimization_barrier(parts)
        total = jnp.sum(parts.astype(jnp.float32), axis=1)
        return total.reshape(LINES, CAPS, D)

    outs = lax.map(one_expert, (jnp.arange(EXPERTS, dtype=jnp.int32), gate_weight, up_weight, down_weight))
    back = jnp.transpose(outs, (1, 0, 2, 3)).reshape(LINES, EXPERTS * CAPS, D)

    def one_line(items):
        table, values, gains, rows = items
        picked = jnp.einsum("skm,md->skd", table, values, precision=lax.Precision.HIGHEST)
        moe = jnp.sum(gains[:, :, None] * picked, axis=1)
        return (rows.astype(jnp.float32) + moe).astype(jnp.bfloat16)

    return lax.map(one_line, (gathers, back, route_gain, hidden_rows))
```

```python
import jax
import jax.numpy as jnp
from jax import lax
from jax.sharding import Mesh, PartitionSpec as P

CHUNK_EDGES = (0, 11, 22, 31, 40)
SCATTER_ORDER = (2, 3, 0, 1)
GAIN_CHUNK = 2
LANES = 128


def expert_tables(info, topk, expert, caps):
    routes, gains = info[:, :topk], info[:, topk:]
    named = (routes == expert.astype(jnp.float32)).astype(jnp.float32)
    count = jnp.sum(named, axis=1)
    gain = jnp.sum(named * gains, axis=1)
    slab = count.shape[1]
    earlier = (jnp.arange(slab)[:, None] < jnp.arange(slab)[None, :]).astype(jnp.float32)
    before = jnp.dot(count, earlier, precision=lax.Precision.HIGHEST)
    grid = jnp.arange(caps).astype(jnp.float32)
    sel = count[:, None, :] * (before[:, None, :] == grid[None, :, None]).astype(jnp.float32)
    return sel, gain


def body(hidden_rows, routes, route_gain, gate_weight, up_weight, down_weight):
    n_lines = lax.axis_size("exp")
    n_grp = lax.axis_size("grp")
    slab, topk = routes.shape[1:]
    caps = min(slab, slab * topk * 4 // (3 * n_lines))
    block = hidden_rows[0]
    half_rows, width = block.shape
    expert = lax.axis_index("exp")

    info = jnp.concatenate([routes[0].astype(jnp.float32), route_gain[0]], axis=1).T
    info = lax.all_gather(info, "exp", axis=0)
    rows = lax.all_gather(block, ("exp", "grp"), axis=0).reshape(n_lines, slab, width)
    sel, gain = expert_tables(info, topk, expert, caps)
    sel = sel.astype(jnp.bfloat16)

    taken = jnp.einsum("lcr,lrd->lcd", sel, rows, preferred_element_type=jnp.float32)
    taken = taken.astype(jnp.bfloat16).reshape(n_lines * caps, width)
    dims = (((1,), (1,)), ((), ()))
    gate = lax.dot_general(taken, gate_weight[0], dims, preferred_element_type=jnp.float32)
    upper = lax.dot_general(taken, up_weight[0], dims, preferred_element_type=jnp.float32)
    gate = lax.psum(gate, "attn")
    upper = lax.psum(upper, "attn")
    act = (jax.nn.silu(gate) * upper).astype(jnp.bfloat16).reshape(n_lines, caps, -1)
    spread = jnp.einsum("lcr,lcf->lrf", sel, act, preferred_element_type=jnp.float32)
    spread = (spread * gain[:, :, None]).astype(jnp.bfloat16).reshape(n_lines * slab, -1)
    part = jnp.dot(spread, down_weight[0], preferred_element_type=jnp.float32).astype(jnp.bfloat16)
    part = part.reshape(n_lines * n_grp, half_rows, width)
    moe = lax.psum_scatter(part, ("exp", "grp"), scatter_dimension=0, tiled=True)[0]
    return (block.astype(jnp.float32) + moe.astype(jnp.float32)).astype(jnp.bfloat16)[None]


NX, NZ, NY, NCORE = 2, 4, 2, 2
AXES = ("x", "z", "y", "core")


def swap(value, axis, flip=1):
    size = {"x": NX, "z": NZ, "y": NY, "core": NCORE}[axis]
    return lax.ppermute(value, axis, [(i, i ^ flip) for i in range(size)])


def after(value, *others):
    return lax.optimization_barrier((value,) + others)[0] if others else value


def gain_columns(routes, route_gain, experts):
    named = routes[:, :, None] == jnp.arange(experts, dtype=jnp.int32)
    rest = jnp.sum(jnp.where(named, route_gain[:, :, None], 0.0), axis=1)
    columns = []
    for _ in range(3):
        piece = lax.reduce_precision(rest, 8, 7)
        columns.append(piece.astype(jnp.bfloat16))
        rest = rest - piece
    columns = jnp.concatenate(columns, axis=1)
    return jnp.pad(columns, ((0, 0), (0, LANES - columns.shape[1])))


def ordered(blocks, y_first):
    return [blocks[0], blocks[2], blocks[1], blocks[3]] if y_first else blocks


def grown(value, *flip):
    return jnp.concatenate([value, swap(value, *flip)], axis=0)


def added(a, b):
    return (a.astype(jnp.float32) + b.astype(jnp.float32)).astype(jnp.bfloat16)


def halved(value, *flip):
    cut = value.shape[0] // 2
    return added(value[:cut], swap(value[cut:], *flip))


def ring_body(hidden_rows, routes, route_gain, gate_weight, up_weight, down_weight):
    n_lines = NZ * NY * NCORE
    block = hidden_rows[0]
    half, width = block.shape
    x, z, y, core = [lax.axis_index(name) for name in AXES]
    expert = (z * NY + y) * NCORE + core
    columns = gain_columns(
        lax.dynamic_slice_in_dim(routes[0], x * half, half, 0),
        lax.dynamic_slice_in_dim(route_gain[0], x * half, half, 0),
        n_lines,
    )
    edges = [width * part // CHUNK_EDGES[-1] for part in CHUNK_EDGES]
    spans = [slice(start, stop) for start, stop in zip(edges, edges[1:])]
    n_chunks = len(spans)
    planes = [("x", "y") if c % 2 == 0 else ("y", "x") for c in range(n_chunks)]
    dims = (((1,), (1,)), ((), ()))

    far, in_z, in_first, received = {}, [], [], []
    for c in range(n_chunks):
        value = block[:, spans[c]]
        if c == GAIN_CHUNK:
            value = jnp.concatenate([value, columns], axis=1)
        if c >= 2:
            value = after(value, *in_z[:2])
        far[c] = grown(value, "z", 2)
        in_z.append(grown(after(far[c], *in_first[:2]) if c >= 2 else far[c], "z", 1))
        value = grown(in_z[c], planes[c][0])
        in_first.append(value)
        if c < 2:
            received.append(swap(value, planes[c][1]))
    joined = lax.optimization_barrier(received + in_first[2:])
    in_first[2:] = joined[2:]
    received = joined[:2] + [swap(in_first[c], planes[c][1]) for c in (2, 3)]

    halves = [{"gate": 0.0, "up": 0.0}, {"gate": 0.0, "up": 0.0}]
    for c in range(n_chunks):
        if c == 2:
            ties = [sums[name] for sums in halves for name in ("gate", "up")]
            received[2:] = lax.optimization_barrier(received[2:] + ties)[:2]
        pieces = jnp.split(in_first[c], 2, axis=0) + jnp.split(received[c], 2, axis=0)
        own = jnp.concatenate(ordered(pieces, c % 2 == 1), axis=0)
        for rows, sums in zip((own, swap(own, "core")), halves):
            if c == GAIN_CHUNK:
                lane = lax.broadcasted_iota(jnp.int32, (rows.shape[0], LANES), 1)
                gains = jnp.where(lax.rem(lane, n_lines) == expert, rows[:, -LANES:].astype(jnp.float32), 0.0)
                sums["gain"] = jnp.sum(gains, axis=1, keepdims=True)
                rows = rows[:, :-LANES]
            for name, weight in (("gate", gate_weight), ("up", up_weight)):
                sums[name] += lax.dot_general(rows, weight[0, :, spans[c]], dims, preferred_element_type=jnp.float32)

    def act(side, *before):
        gate, upper = after(halves[side]["gate"], *before), halves[side]["up"]
        value = (jax.nn.silu(gate) * upper * halves[side]["gain"]).astype(jnp.bfloat16)
        return lax.optimization_barrier(value)

    def down(value, c):
        return jnp.dot(value, down_weight[0, :, spans[c]], preferred_element_type=jnp.float32)

    away = act(1)
    to_core = {c: down(away, c).astype(jnp.bfloat16) for c in SCATTER_ORDER[:2]}
    here = act(0, *to_core.values())
    away = after(away, *to_core.values())
    to_core.update({c: down(away, c).astype(jnp.bfloat16) for c in SCATTER_ORDER[2:]})
    parts, sent, kept = {}, {}, {}
    for c in SCATTER_ORDER:
        part = (down(here, c) + swap(to_core[c], "core").astype(jnp.float32)).astype(jnp.bfloat16)
        parts[c] = jnp.concatenate(ordered(jnp.split(part, 4, axis=0), c % 2 == 1), axis=0)
        kept[c], goes = jnp.split(parts[c], 2, axis=0)
        sent[c] = swap(goes, planes[c][1])
    following = {c: SCATTER_ORDER[i + 2 - i % 2:i + 4 - i % 2] for i, c in enumerate(SCATTER_ORDER)}
    outs, first = {}, {}
    for c in SCATTER_ORDER:
        first[c] = added(kept[c], after(sent[c], *[parts[d] for d in following[c]]))
    for c in SCATTER_ORDER:
        stays, goes = jnp.split(first[c], 2, axis=0)
        part = added(stays, after(swap(goes, planes[c][0]), *[first[d] for d in following[c]]))
        part = halved(part, "z", 1)
        total = block[:, spans[c]].astype(jnp.float32) + part[:half].astype(jnp.float32)
        total += swap(part[half:], "z", 2).astype(jnp.float32)
        outs[c] = total.astype(jnp.bfloat16)
    return jnp.concatenate([outs[c] for c in range(n_chunks)], axis=1)[None]


def solution(mesh):
    small = dict(mesh.shape) == {"grp": NX, "attn": 1, "exp": NZ * NY * NCORE}
    if small:
        mesh = Mesh(mesh.devices.reshape(NX, NZ, NY, NCORE), AXES)
        exp, grp, attn, run = ("z", "y", "core"), "x", None, ring_body
    else:
        exp, grp, attn, run = "exp", "grp", "attn", body
    placed = (
        P(exp, grp, attn),
        P(exp, None, None),
        P(exp, None, None),
        P(exp, grp, attn),
        P(exp, grp, attn),
        P(exp, grp, attn),
    )
    return jax.shard_map(run, mesh=mesh, in_specs=placed, out_specs=P(exp, grp, attn), check_vma=False)
```

```python
import jax
import jax.numpy as jnp
from jax import lax
from jax.sharding import Mesh, PartitionSpec as P

CHUNK_EDGES = (0, 11, 22, 31, 40)
GAIN_CHUNK = 2
LANES = 128


def expert_tables(info, topk, expert, caps):
    routes, gains = info[:, :topk], info[:, topk:]
    named = (routes == expert.astype(jnp.float32)).astype(jnp.float32)
    count = jnp.sum(named, axis=1)
    gain = jnp.sum(named * gains, axis=1)
    slab = count.shape[1]
    earlier = (jnp.arange(slab)[:, None] < jnp.arange(slab)[None, :]).astype(jnp.float32)
    before = jnp.dot(count, earlier, precision=lax.Precision.HIGHEST)
    grid = jnp.arange(caps).astype(jnp.float32)
    sel = count[:, None, :] * (before[:, None, :] == grid[None, :, None]).astype(jnp.float32)
    return sel, gain


def body(hidden_rows, routes, route_gain, gate_weight, up_weight, down_weight):
    n_lines = lax.axis_size("exp")
    n_grp = lax.axis_size("grp")
    slab, topk = routes.shape[1:]
    caps = min(slab, slab * topk * 4 // (3 * n_lines))
    block = hidden_rows[0]
    half_rows, width = block.shape
    expert = lax.axis_index("exp")

    info = jnp.concatenate([routes[0].astype(jnp.float32), route_gain[0]], axis=1).T
    info = lax.all_gather(info, "exp", axis=0)
    rows = lax.all_gather(block, ("exp", "grp"), axis=0).reshape(n_lines, slab, width)
    sel, gain = expert_tables(info, topk, expert, caps)
    sel = sel.astype(jnp.bfloat16)

    taken = jnp.einsum("lcr,lrd->lcd", sel, rows, preferred_element_type=jnp.float32)
    taken = taken.astype(jnp.bfloat16).reshape(n_lines * caps, width)
    dims = (((1,), (1,)), ((), ()))
    gate = lax.dot_general(taken, gate_weight[0], dims, preferred_element_type=jnp.float32)
    upper = lax.dot_general(taken, up_weight[0], dims, preferred_element_type=jnp.float32)
    gate = lax.psum(gate, "attn")
    upper = lax.psum(upper, "attn")
    act = (jax.nn.silu(gate) * upper).astype(jnp.bfloat16).reshape(n_lines, caps, -1)
    spread = jnp.einsum("lcr,lcf->lrf", sel, act, preferred_element_type=jnp.float32)
    spread = (spread * gain[:, :, None]).astype(jnp.bfloat16).reshape(n_lines * slab, -1)
    part = jnp.dot(spread, down_weight[0], preferred_element_type=jnp.float32).astype(jnp.bfloat16)
    part = part.reshape(n_lines * n_grp, half_rows, width)
    moe = lax.psum_scatter(part, ("exp", "grp"), scatter_dimension=0, tiled=True)[0]
    return (block.astype(jnp.float32) + moe.astype(jnp.float32)).astype(jnp.bfloat16)[None]


NX, NZ, NY, NCORE = 2, 4, 2, 2
AXES = ("x", "z", "y", "core")


def swap(value, axis, flip=1):
    size = {"x": NX, "z": NZ, "y": NY, "core": NCORE}[axis]
    return lax.ppermute(value, axis, [(i, i ^ flip) for i in range(size)])


def after(value, *others):
    return lax.optimization_barrier((value,) + others)[0] if others else value


def gain_columns(routes, route_gain, experts):
    named = routes[:, :, None] == jnp.arange(experts, dtype=jnp.int32)
    rest = jnp.sum(jnp.where(named, route_gain[:, :, None], 0.0), axis=1)
    columns = []
    for _ in range(3):
        piece = lax.reduce_precision(rest, 8, 7)
        columns.append(piece.astype(jnp.bfloat16))
        rest = rest - piece
    columns = jnp.concatenate(columns, axis=1)
    return jnp.pad(columns, ((0, 0), (0, LANES - columns.shape[1])))


FAR, NEAR = ("z", 2), ("z", 1)
STAGES = (
    (FAR, NEAR, ("x",), ("y",)),
    (FAR, NEAR, ("y",), ("x",)),
    (("x",), FAR, NEAR, ("y",)),
    (("y",), FAR, NEAR, ("x",)),
)


def ordered(value, old, new):
    if old == new:
        return value
    blocks = value.reshape((2,) * len(old) + (-1, value.shape[1]))
    axes = [old[::-1].index(flip) for flip in new[::-1]]
    return jnp.transpose(blocks, axes + [len(old), len(old) + 1]).reshape(value.shape)


def grown(value, flip):
    return jnp.concatenate([value, swap(value, *flip)], axis=0)


def added(a, b):
    return (a.astype(jnp.float32) + b.astype(jnp.float32)).astype(jnp.bfloat16)


def halved(value, flip):
    cut = value.shape[0] // 2
    return added(value[:cut], swap(value[cut:], *flip))


def ring_body(hidden_rows, routes, route_gain, gate_weight, up_weight, down_weight):
    n_lines = NZ * NY * NCORE
    block = hidden_rows[0]
    half, width = block.shape
    x, z, y, core = [lax.axis_index(name) for name in AXES]
    expert = (z * NY + y) * NCORE + core
    columns = gain_columns(
        lax.dynamic_slice_in_dim(routes[0], x * half, half, 0),
        lax.dynamic_slice_in_dim(route_gain[0], x * half, half, 0),
        n_lines,
    )
    edges = [width * part // CHUNK_EDGES[-1] for part in CHUNK_EDGES]
    spans = [slice(start, stop) for start, stop in zip(edges, edges[1:])]
    n_chunks = len(spans)
    dims = (((1,), (1,)), ((), ()))

    chunks = [block[:, span] for span in spans]
    one, two = (0, 1), (2, 3)
    in_far = [grown(chunks[c], FAR) for c in one]
    in_z = [grown(value, NEAR) for value in in_far]
    before_last = [grown(value, STAGES[c][2]) for c, value in zip(one, in_z)]
    flipped = [grown(after(chunks[c], *in_far), STAGES[c][0]) for c in two]
    at = GAIN_CHUNK - two[0]
    flipped[at] = jnp.concatenate([flipped[at], grown(after(columns, *in_far), STAGES[GAIN_CHUNK][0])], axis=1)
    far = [grown(after(value, *in_z), FAR) for value in flipped]
    near = [grown(after(value, *before_last), NEAR) for value in far]
    received = [swap(value, *STAGES[c][3]) for c, value in zip(one, before_last)]
    joined = lax.optimization_barrier(received + near)
    before_last += joined[2:]
    received = joined[:2] + [swap(before_last[c], *STAGES[c][3]) for c in two]

    halves = [{"gate": 0.0, "up": 0.0}, {"gate": 0.0, "up": 0.0}]
    for c in range(n_chunks):
        if c == 2:
            ties = [sums[name] for sums in halves for name in ("gate", "up")]
            received[2:] = lax.optimization_barrier(received[2:] + ties)[:2]
        own = ordered(jnp.concatenate([before_last[c], received[c]], axis=0), STAGES[c], STAGES[0])
        for rows, sums in zip((own, swap(own, "core")), halves):
            if c == GAIN_CHUNK:
                lane = lax.broadcasted_iota(jnp.int32, (rows.shape[0], LANES), 1)
                gains = jnp.where(lax.rem(lane, n_lines) == expert, rows[:, -LANES:].astype(jnp.float32), 0.0)
                sums["gain"] = jnp.sum(gains, axis=1, keepdims=True)
                rows = rows[:, :-LANES]
            for name, weight in (("gate", gate_weight), ("up", up_weight)):
                sums[name] += lax.dot_general(rows, weight[0, :, spans[c]], dims, preferred_element_type=jnp.float32)

    def act(side, *before):
        gate, upper = after(halves[side]["gate"], *before), halves[side]["up"]
        value = (jax.nn.silu(gate) * upper * halves[side]["gain"]).astype(jnp.bfloat16)
        return lax.optimization_barrier(value)

    def down(value, c):
        return jnp.dot(value, down_weight[0, :, spans[c]], preferred_element_type=jnp.float32)

    away = act(1)
    to_core = {c: down(ordered(away, STAGES[0], STAGES[c]), c).astype(jnp.bfloat16) for c in two}
    here = act(0, *to_core.values())
    away = after(away, *to_core.values())
    to_core.update({c: down(ordered(away, STAGES[0], STAGES[c]), c).astype(jnp.bfloat16) for c in one})
    parts, kept, sent = {}, {}, {}
    for c in two + one:
        parts[c] = added(down(ordered(here, STAGES[0], STAGES[c]), c), swap(to_core[c], "core"))
        kept[c], goes = jnp.split(parts[c], 2, axis=0)
        sent[c] = swap(goes, *STAGES[c][3])
    first = {c: added(kept[c], sent[c]) for c in one}
    outs = {}
    for c in two:
        value = halved(added(kept[c], after(sent[c], *[parts[d] for d in one])), NEAR)
        stays, goes = jnp.split(value, 2, axis=0)
        value = added(stays, after(swap(goes, *FAR), *first.values()))
        outs[c] = (value, STAGES[c][0])
    for c in one:
        outs[c] = (halved(halved(first[c], STAGES[c][2]), NEAR), FAR)
    for c, (value, flip) in outs.items():
        total = block[:, spans[c]].astype(jnp.float32) + value[:half].astype(jnp.float32)
        outs[c] = (total + swap(value[half:], *flip).astype(jnp.float32)).astype(jnp.bfloat16)
    return jnp.concatenate([outs[c] for c in range(n_chunks)], axis=1)[None]


def solution(mesh):
    small = dict(mesh.shape) == {"grp": NX, "attn": 1, "exp": NZ * NY * NCORE}
    if small:
        mesh = Mesh(mesh.devices.reshape(NX, NZ, NY, NCORE), AXES)
        exp, grp, attn, run = ("z", "y", "core"), "x", None, ring_body
    else:
        exp, grp, attn, run = "exp", "grp", "attn", body
    placed = (
        P(exp, grp, attn),
        P(exp, None, None),
        P(exp, None, None),
        P(exp, grp, attn),
        P(exp, grp, attn),
        P(exp, grp, attn),
    )
    return jax.shard_map(run, mesh=mesh, in_specs=placed, out_specs=P(exp, grp, attn), check_vma=False)
```

```python
import jax
import jax.numpy as jnp
from jax import lax
from jax.sharding import Mesh, PartitionSpec as P

GATHER_EDGES = (0, 12, 24, 32, 40)
SCATTER_EDGES = (0, 11, 22, 31, 40)
GAIN_CHUNK = 2
LANES = 128


def expert_tables(info, topk, expert, caps):
    routes, gains = info[:, :topk], info[:, topk:]
    named = (routes == expert.astype(jnp.float32)).astype(jnp.float32)
    count = jnp.sum(named, axis=1)
    gain = jnp.sum(named * gains, axis=1)
    slab = count.shape[1]
    earlier = (jnp.arange(slab)[:, None] < jnp.arange(slab)[None, :]).astype(jnp.float32)
    before = jnp.dot(count, earlier, precision=lax.Precision.HIGHEST)
    grid = jnp.arange(caps).astype(jnp.float32)
    sel = count[:, None, :] * (before[:, None, :] == grid[None, :, None]).astype(jnp.float32)
    return sel, gain


def body(hidden_rows, routes, route_gain, gate_weight, up_weight, down_weight):
    n_lines = lax.axis_size("exp")
    n_grp = lax.axis_size("grp")
    slab, topk = routes.shape[1:]
    caps = min(slab, slab * topk * 4 // (3 * n_lines))
    block = hidden_rows[0]
    half_rows, width = block.shape
    expert = lax.axis_index("exp")

    info = jnp.concatenate([routes[0].astype(jnp.float32), route_gain[0]], axis=1).T
    info = lax.all_gather(info, "exp", axis=0)
    rows = lax.all_gather(block, ("exp", "grp"), axis=0).reshape(n_lines, slab, width)
    sel, gain = expert_tables(info, topk, expert, caps)
    sel = sel.astype(jnp.bfloat16)

    taken = jnp.einsum("lcr,lrd->lcd", sel, rows, preferred_element_type=jnp.float32)
    taken = taken.astype(jnp.bfloat16).reshape(n_lines * caps, width)
    dims = (((1,), (1,)), ((), ()))
    gate = lax.dot_general(taken, gate_weight[0], dims, preferred_element_type=jnp.float32)
    upper = lax.dot_general(taken, up_weight[0], dims, preferred_element_type=jnp.float32)
    gate = lax.psum(gate, "attn")
    upper = lax.psum(upper, "attn")
    act = (jax.nn.silu(gate) * upper).astype(jnp.bfloat16).reshape(n_lines, caps, -1)
    spread = jnp.einsum("lcr,lcf->lrf", sel, act, preferred_element_type=jnp.float32)
    spread = (spread * gain[:, :, None]).astype(jnp.bfloat16).reshape(n_lines * slab, -1)
    part = jnp.dot(spread, down_weight[0], preferred_element_type=jnp.float32).astype(jnp.bfloat16)
    part = part.reshape(n_lines * n_grp, half_rows, width)
    moe = lax.psum_scatter(part, ("exp", "grp"), scatter_dimension=0, tiled=True)[0]
    return (block.astype(jnp.float32) + moe.astype(jnp.float32)).astype(jnp.bfloat16)[None]


NX, NZ, NY, NCORE = 2, 4, 2, 2
AXES = ("x", "z", "y", "core")


def swap(value, axis, flip=1):
    size = {"x": NX, "z": NZ, "y": NY, "core": NCORE}[axis]
    return lax.ppermute(value, axis, [(i, i ^ flip) for i in range(size)])


def after(value, *others):
    return lax.optimization_barrier((value,) + others)[0] if others else value


def gain_columns(routes, route_gain, experts):
    named = routes[:, :, None] == jnp.arange(experts, dtype=jnp.int32)
    rest = jnp.sum(jnp.where(named, route_gain[:, :, None], 0.0), axis=1)
    columns = []
    for _ in range(3):
        piece = lax.reduce_precision(rest, 8, 7)
        columns.append(piece.astype(jnp.bfloat16))
        rest = rest - piece
    columns = jnp.concatenate(columns, axis=1)
    return jnp.pad(columns, ((0, 0), (0, LANES - columns.shape[1])))


FAR, NEAR = ("z", 2), ("z", 1)
STAGES = (
    (FAR, NEAR, ("x",), ("y",)),
    (FAR, NEAR, ("y",), ("x",)),
    (("x",), FAR, NEAR, ("y",)),
    (("y",), FAR, NEAR, ("x",)),
)


def ordered(value, old, new):
    if old == new:
        return value
    blocks = value.reshape((2,) * len(old) + (-1, value.shape[1]))
    axes = [old[::-1].index(flip) for flip in new[::-1]]
    return jnp.transpose(blocks, axes + [len(old), len(old) + 1]).reshape(value.shape)


def grown(value, flip):
    return jnp.concatenate([value, swap(value, *flip)], axis=0)


def added(a, b):
    return (a.astype(jnp.float32) + b.astype(jnp.float32)).astype(jnp.bfloat16)


def halved(value, flip):
    cut = value.shape[0] // 2
    return added(value[:cut], swap(value[cut:], *flip))


def ring_body(hidden_rows, routes, route_gain, gate_weight, up_weight, down_weight):
    n_lines = NZ * NY * NCORE
    block = hidden_rows[0]
    half, width = block.shape
    x, z, y, core = [lax.axis_index(name) for name in AXES]
    expert = (z * NY + y) * NCORE + core
    columns = gain_columns(
        lax.dynamic_slice_in_dim(routes[0], x * half, half, 0),
        lax.dynamic_slice_in_dim(route_gain[0], x * half, half, 0),
        n_lines,
    )

    def cut(edges):
        edges = [width * part // edges[-1] for part in edges]
        return [slice(start, stop) for start, stop in zip(edges, edges[1:])]

    spans, back_spans = cut(GATHER_EDGES), cut(SCATTER_EDGES)
    n_chunks = len(spans)
    dims = (((1,), (1,)), ((), ()))

    chunks = [block[:, span] for span in spans]
    one, two = (0, 1), (2, 3)
    in_far = [grown(chunks[c], FAR) for c in one]
    in_z = [grown(value, NEAR) for value in in_far]
    before_last = [grown(value, STAGES[c][2]) for c, value in zip(one, in_z)]
    flipped = [grown(after(chunks[c], *in_far), STAGES[c][0]) for c in two]
    at = GAIN_CHUNK - two[0]
    flipped[at] = jnp.concatenate([flipped[at], grown(after(columns, *in_far), STAGES[GAIN_CHUNK][0])], axis=1)
    flipped = [after(value, *in_z) for value in flipped]
    far = [jnp.concatenate([value, after(swap(value, *FAR), *before_last)], axis=0) for value in flipped]
    near = [grown(value, NEAR) for value in far]
    received = [swap(value, *STAGES[c][3]) for c, value in zip(one, before_last)]
    joined = lax.optimization_barrier(received + near)
    before_last += joined[2:]
    received = joined[:2] + [swap(before_last[c], *STAGES[c][3]) for c in two]

    halves = [{"gate": 0.0, "up": 0.0}, {"gate": 0.0, "up": 0.0}]
    for c in range(n_chunks):
        if c == 2:
            ties = [sums[name] for sums in halves for name in ("gate", "up")]
            received[2:] = lax.optimization_barrier(received[2:] + ties)[:2]
        own = ordered(jnp.concatenate([before_last[c], received[c]], axis=0), STAGES[c], STAGES[0])
        for rows, sums in zip((own, swap(own, "core")), halves):
            if c == GAIN_CHUNK:
                lane = lax.broadcasted_iota(jnp.int32, (rows.shape[0], LANES), 1)
                gains = jnp.where(lax.rem(lane, n_lines) == expert, rows[:, -LANES:].astype(jnp.float32), 0.0)
                sums["gain"] = jnp.sum(gains, axis=1, keepdims=True)
                rows = rows[:, :-LANES]
            for name, weight in (("gate", gate_weight), ("up", up_weight)):
                sums[name] += lax.dot_general(rows, weight[0, :, spans[c]], dims, preferred_element_type=jnp.float32)

    def act(side, *before):
        gate, upper = after(halves[side]["gate"], *before), halves[side]["up"]
        value = (jax.nn.silu(gate) * upper * halves[side]["gain"]).astype(jnp.bfloat16)
        return lax.optimization_barrier(value)

    def down(value, c):
        return jnp.dot(value, down_weight[0, :, back_spans[c]], preferred_element_type=jnp.float32)

    away = act(1)
    to_core = {c: down(ordered(away, STAGES[0], STAGES[c]), c).astype(jnp.bfloat16) for c in two}
    here = act(0, *to_core.values())
    away = after(away, *to_core.values())
    to_core.update({c: down(ordered(away, STAGES[0], STAGES[c]), c).astype(jnp.bfloat16) for c in one})
    parts, kept, sent = {}, {}, {}
    for c in two + one:
        parts[c] = added(down(ordered(here, STAGES[0], STAGES[c]), c), swap(to_core[c], "core"))
        kept[c], goes = jnp.split(parts[c], 2, axis=0)
        sent[c] = swap(goes, *STAGES[c][3])
    first = {c: added(kept[c], sent[c]) for c in one}
    outs = {}
    for c in two:
        value = halved(added(kept[c], after(sent[c], *[parts[d] for d in one])), NEAR)
        stays, goes = jnp.split(value, 2, axis=0)
        value = added(stays, after(swap(goes, *FAR), *first.values()))
        outs[c] = (value, STAGES[c][0])
    for c in one:
        outs[c] = (halved(halved(first[c], STAGES[c][2]), NEAR), FAR)
    for c, (value, flip) in outs.items():
        total = block[:, back_spans[c]].astype(jnp.float32) + value[:half].astype(jnp.float32)
        outs[c] = (total + swap(value[half:], *flip).astype(jnp.float32)).astype(jnp.bfloat16)
    return jnp.concatenate([outs[c] for c in range(n_chunks)], axis=1)[None]


def solution(mesh):
    small = dict(mesh.shape) == {"grp": NX, "attn": 1, "exp": NZ * NY * NCORE}
    if small:
        mesh = Mesh(mesh.devices.reshape(NX, NZ, NY, NCORE), AXES)
        exp, grp, attn, run = ("z", "y", "core"), "x", None, ring_body
    else:
        exp, grp, attn, run = "exp", "grp", "attn", body
    placed = (
        P(exp, grp, attn),
        P(exp, None, None),
        P(exp, None, None),
        P(exp, grp, attn),
        P(exp, grp, attn),
        P(exp, grp, attn),
    )
    return jax.shard_map(run, mesh=mesh, in_specs=placed, out_specs=P(exp, grp, attn), check_vma=False)
```

```python
import jax
import jax.numpy as jnp
from jax import lax
from jax.sharding import Mesh, PartitionSpec as P

GATHER_EDGES = (0, 12, 24, 32, 40)
SCATTER_EDGES = (0, 11, 22, 31, 40)
GAIN_CHUNK = 2
LANES = 128


def expert_tables(info, topk, expert, caps):
    routes, gains = info[:, :topk], info[:, topk:]
    named = (routes == expert.astype(jnp.float32)).astype(jnp.float32)
    count = jnp.sum(named, axis=1)
    gain = jnp.sum(named * gains, axis=1)
    slab = count.shape[1]
    earlier = (jnp.arange(slab)[:, None] < jnp.arange(slab)[None, :]).astype(jnp.float32)
    before = jnp.dot(count, earlier, precision=lax.Precision.HIGHEST)
    grid = jnp.arange(caps).astype(jnp.float32)
    sel = count[:, None, :] * (before[:, None, :] == grid[None, :, None]).astype(jnp.float32)
    return sel, gain


def body(hidden_rows, routes, route_gain, gate_weight, up_weight, down_weight):
    n_lines = lax.axis_size("exp")
    n_grp = lax.axis_size("grp")
    slab, topk = routes.shape[1:]
    caps = min(slab, slab * topk * 4 // (3 * n_lines))
    block = hidden_rows[0]
    half_rows, width = block.shape
    expert = lax.axis_index("exp")

    info = jnp.concatenate([routes[0].astype(jnp.float32), route_gain[0]], axis=1).T
    info = lax.all_gather(info, "exp", axis=0)
    rows = lax.all_gather(block, ("exp", "grp"), axis=0).reshape(n_lines, slab, width)
    sel, gain = expert_tables(info, topk, expert, caps)
    sel = sel.astype(jnp.bfloat16)

    taken = jnp.einsum("lcr,lrd->lcd", sel, rows, preferred_element_type=jnp.float32)
    taken = taken.astype(jnp.bfloat16).reshape(n_lines * caps, width)
    dims = (((1,), (1,)), ((), ()))
    gate = lax.dot_general(taken, gate_weight[0], dims, preferred_element_type=jnp.float32)
    upper = lax.dot_general(taken, up_weight[0], dims, preferred_element_type=jnp.float32)
    gate = lax.psum(gate, "attn")
    upper = lax.psum(upper, "attn")
    act = (jax.nn.silu(gate) * upper).astype(jnp.bfloat16).reshape(n_lines, caps, -1)
    spread = jnp.einsum("lcr,lcf->lrf", sel, act, preferred_element_type=jnp.float32)
    spread = (spread * gain[:, :, None]).astype(jnp.bfloat16).reshape(n_lines * slab, -1)
    part = jnp.dot(spread, down_weight[0], preferred_element_type=jnp.float32).astype(jnp.bfloat16)
    part = part.reshape(n_lines * n_grp, half_rows, width)
    moe = lax.psum_scatter(part, ("exp", "grp"), scatter_dimension=0, tiled=True)[0]
    return (block.astype(jnp.float32) + moe.astype(jnp.float32)).astype(jnp.bfloat16)[None]


NX, NZ, NY, NCORE = 2, 4, 2, 2
AXES = ("x", "z", "y", "core")


def swap(value, axis, flip=1):
    size = {"x": NX, "z": NZ, "y": NY, "core": NCORE}[axis]
    return lax.ppermute(value, axis, [(i, i ^ flip) for i in range(size)])


def after(value, *others):
    return lax.optimization_barrier((value,) + others)[0] if others else value


def gain_columns(routes, route_gain, experts):
    named = routes[:, :, None] == jnp.arange(experts, dtype=jnp.int32)
    rest = jnp.sum(jnp.where(named, route_gain[:, :, None], 0.0), axis=1)
    columns = []
    for _ in range(3):
        piece = lax.reduce_precision(rest, 8, 7)
        columns.append(piece.astype(jnp.bfloat16))
        rest = rest - piece
    columns = jnp.concatenate(columns, axis=1)
    return jnp.pad(columns, ((0, 0), (0, LANES - columns.shape[1])))


FAR, NEAR = ("z", 2), ("z", 1)
STAGES = (
    (FAR, NEAR, ("x",), ("y",)),
    (FAR, NEAR, ("y",), ("x",)),
    (("x",), FAR, NEAR, ("y",)),
    (("y",), FAR, NEAR, ("x",)),
)


def ordered(value, old, new):
    if old == new:
        return value
    blocks = value.reshape((2,) * len(old) + (-1, value.shape[1]))
    axes = [old[::-1].index(flip) for flip in new[::-1]]
    return jnp.transpose(blocks, axes + [len(old), len(old) + 1]).reshape(value.shape)


def grown(value, flip):
    return jnp.concatenate([value, swap(value, *flip)], axis=0)


def added(a, b):
    return (a.astype(jnp.float32) + b.astype(jnp.float32)).astype(jnp.bfloat16)


def halved(value, flip):
    cut = value.shape[0] // 2
    return added(value[:cut], swap(value[cut:], *flip))


def ring_body(hidden_rows, routes, route_gain, gate_weight, up_weight, down_weight):
    n_lines = NZ * NY * NCORE
    block = hidden_rows[0]
    half, width = block.shape
    x, z, y, core = [lax.axis_index(name) for name in AXES]
    expert = (z * NY + y) * NCORE + core
    columns = gain_columns(
        lax.dynamic_slice_in_dim(routes[0], x * half, half, 0),
        lax.dynamic_slice_in_dim(route_gain[0], x * half, half, 0),
        n_lines,
    )

    def cut(edges):
        edges = [width * part // edges[-1] for part in edges]
        return [slice(start, stop) for start, stop in zip(edges, edges[1:])]

    spans, back_spans = cut(GATHER_EDGES), cut(SCATTER_EDGES)
    n_chunks = len(spans)
    dims = (((1,), (1,)), ((), ()))

    chunks = [block[:, span] for span in spans]
    one, two = (0, 1), (2, 3)
    in_far = [grown(chunks[c], FAR) for c in one]
    in_z = [grown(value, NEAR) for value in in_far]
    before_last = [grown(value, STAGES[c][2]) for c, value in zip(one, in_z)]
    flipped = [grown(after(chunks[c], *in_far), STAGES[c][0]) for c in two]
    at = GAIN_CHUNK - two[0]
    flipped[at] = jnp.concatenate([flipped[at], grown(after(columns, *in_far), STAGES[GAIN_CHUNK][0])], axis=1)
    flipped = [after(value, *in_z) for value in flipped]
    far = [jnp.concatenate([value, after(swap(value, *FAR), *before_last)], axis=0) for value in flipped]
    near = [grown(value, NEAR) for value in far]
    received = [swap(value, *STAGES[c][3]) for c, value in zip(one, before_last)]
    joined = lax.optimization_barrier(received + near)
    before_last += joined[2:]
    received = joined[:2] + [swap(before_last[c], *STAGES[c][3]) for c in two]

    halves = [{"gate": 0.0, "up": 0.0}, {"gate": 0.0, "up": 0.0}]
    for c in range(n_chunks):
        if c == 1:
            partial = halves[1]["up"]
        if c == 2:
            ties = [halves[0]["gate"], halves[0]["up"], halves[1]["gate"], partial]
            received[2:] = lax.optimization_barrier(received[2:] + ties)[:2]
        own = ordered(jnp.concatenate([before_last[c], received[c]], axis=0), STAGES[c], STAGES[0])
        for rows, sums in zip((own, swap(own, "core")), halves):
            if c == GAIN_CHUNK:
                lane = lax.broadcasted_iota(jnp.int32, (rows.shape[0], LANES), 1)
                gains = jnp.where(lax.rem(lane, n_lines) == expert, rows[:, -LANES:].astype(jnp.float32), 0.0)
                sums["gain"] = jnp.sum(gains, axis=1, keepdims=True)
                rows = rows[:, :-LANES]
            for name, weight in (("gate", gate_weight), ("up", up_weight)):
                sums[name] += lax.dot_general(rows, weight[0, :, spans[c]], dims, preferred_element_type=jnp.float32)

    def act(side, *before):
        gate, upper = after(halves[side]["gate"], *before), halves[side]["up"]
        value = (jax.nn.silu(gate) * upper * halves[side]["gain"]).astype(jnp.bfloat16)
        return lax.optimization_barrier(value)

    def down(value, c):
        return jnp.dot(value, down_weight[0, :, back_spans[c]], preferred_element_type=jnp.float32)

    away = act(1)
    to_core = {c: down(ordered(away, STAGES[0], STAGES[c]), c).astype(jnp.bfloat16) for c in two}
    here = act(0, *to_core.values())
    away = after(away, *to_core.values())
    to_core.update({c: down(ordered(away, STAGES[0], STAGES[c]), c).astype(jnp.bfloat16) for c in one})
    parts, kept, sent = {}, {}, {}
    for c in two + one:
        parts[c] = added(down(ordered(here, STAGES[0], STAGES[c]), c), swap(to_core[c], "core"))
        kept[c], goes = jnp.split(parts[c], 2, axis=0)
        sent[c] = swap(goes, *STAGES[c][3])
    first = {c: added(kept[c], sent[c]) for c in one}
    outs = {}
    for c in two:
        value = added(kept[c], after(sent[c], *[parts[d] for d in one]))
        stays, goes = jnp.split(value, 2, axis=0)
        goes = swap(goes, *NEAR)
        value = added(stays, after(goes, *first.values()) if c == two[0] else goes)
        stays, goes = jnp.split(value, 2, axis=0)
        value = added(stays, after(swap(goes, *FAR), *first.values()))
        outs[c] = (value, STAGES[c][0])
    for c in one:
        outs[c] = (halved(halved(first[c], STAGES[c][2]), NEAR), FAR)
    for c, (value, flip) in outs.items():
        total = block[:, back_spans[c]].astype(jnp.float32) + value[:half].astype(jnp.float32)
        outs[c] = (total + swap(value[half:], *flip).astype(jnp.float32)).astype(jnp.bfloat16)
    return jnp.concatenate([outs[c] for c in range(n_chunks)], axis=1)[None]


def solution(mesh):
    small = dict(mesh.shape) == {"grp": NX, "attn": 1, "exp": NZ * NY * NCORE}
    if small:
        mesh = Mesh(mesh.devices.reshape(NX, NZ, NY, NCORE), AXES)
        exp, grp, attn, run = ("z", "y", "core"), "x", None, ring_body
    else:
        exp, grp, attn, run = "exp", "grp", "attn", body
    placed = (
        P(exp, grp, attn),
        P(exp, None, None),
        P(exp, None, None),
        P(exp, grp, attn),
        P(exp, grp, attn),
        P(exp, grp, attn),
    )
    return jax.shard_map(run, mesh=mesh, in_specs=placed, out_specs=P(exp, grp, attn), check_vma=False)
```

```python
import jax
import jax.numpy as jnp
from jax import lax
from jax.sharding import Mesh, PartitionSpec as P

GATHER_EDGES = (0, 12, 24, 32, 40)
SCATTER_EDGES = (0, 11, 22, 31, 40)
GAIN_CHUNK = 2
LANES = 128


def expert_tables(info, topk, expert, caps):
    routes, gains = info[:, :topk], info[:, topk:]
    named = (routes == expert.astype(jnp.float32)).astype(jnp.float32)
    count = jnp.sum(named, axis=1)
    gain = jnp.sum(named * gains, axis=1)
    slab = count.shape[1]
    earlier = (jnp.arange(slab)[:, None] < jnp.arange(slab)[None, :]).astype(jnp.float32)
    before = jnp.dot(count, earlier, precision=lax.Precision.HIGHEST)
    grid = jnp.arange(caps).astype(jnp.float32)
    sel = count[:, None, :] * (before[:, None, :] == grid[None, :, None]).astype(jnp.float32)
    return sel, gain


def body(hidden_rows, routes, route_gain, gate_weight, up_weight, down_weight):
    n_lines = lax.axis_size("exp")
    n_grp = lax.axis_size("grp")
    slab, topk = routes.shape[1:]
    caps = min(slab, slab * topk * 4 // (3 * n_lines))
    block = hidden_rows[0]
    half_rows, width = block.shape
    expert = lax.axis_index("exp")

    info = jnp.concatenate([routes[0].astype(jnp.float32), route_gain[0]], axis=1).T
    info = lax.all_gather(info, "exp", axis=0)
    rows = lax.all_gather(block, ("exp", "grp"), axis=0).reshape(n_lines, slab, width)
    sel, gain = expert_tables(info, topk, expert, caps)
    sel = sel.astype(jnp.bfloat16)

    taken = jnp.einsum("lcr,lrd->lcd", sel, rows, preferred_element_type=jnp.float32)
    taken = taken.astype(jnp.bfloat16).reshape(n_lines * caps, width)
    dims = (((1,), (1,)), ((), ()))
    gate = lax.dot_general(taken, gate_weight[0], dims, preferred_element_type=jnp.float32)
    upper = lax.dot_general(taken, up_weight[0], dims, preferred_element_type=jnp.float32)
    gate = lax.psum(gate, "attn")
    upper = lax.psum(upper, "attn")
    act = (jax.nn.silu(gate) * upper).astype(jnp.bfloat16).reshape(n_lines, caps, -1)
    spread = jnp.einsum("lcr,lcf->lrf", sel, act, preferred_element_type=jnp.float32)
    spread = (spread * gain[:, :, None]).astype(jnp.bfloat16).reshape(n_lines * slab, -1)
    part = jnp.dot(spread, down_weight[0], preferred_element_type=jnp.float32).astype(jnp.bfloat16)
    part = part.reshape(n_lines * n_grp, half_rows, width)
    moe = lax.psum_scatter(part, ("exp", "grp"), scatter_dimension=0, tiled=True)[0]
    return (block.astype(jnp.float32) + moe.astype(jnp.float32)).astype(jnp.bfloat16)[None]


NX, NZ, NY, NCORE = 2, 4, 2, 2
AXES = ("x", "z", "y", "core")


def swap(value, axis, flip=1):
    size = {"x": NX, "z": NZ, "y": NY, "core": NCORE}[axis]
    return lax.ppermute(value, axis, [(i, i ^ flip) for i in range(size)])


def after(value, *others):
    return lax.optimization_barrier((value,) + others)[0] if others else value


def gain_columns(routes, route_gain, experts):
    named = routes[:, :, None] == jnp.arange(experts, dtype=jnp.int32)
    rest = jnp.sum(jnp.where(named, route_gain[:, :, None], 0.0), axis=1)
    columns = []
    for _ in range(3):
        piece = lax.reduce_precision(rest, 8, 7)
        columns.append(piece.astype(jnp.bfloat16))
        rest = rest - piece
    columns = jnp.concatenate(columns, axis=1)
    return jnp.pad(columns, ((0, 0), (0, LANES - columns.shape[1])))


FAR, NEAR = ("z", 2), ("z", 1)
STAGES = (
    (FAR, NEAR, ("x",), ("y",)),
    (FAR, NEAR, ("y",), ("x",)),
    (("x",), FAR, NEAR, ("y",)),
    (("y",), FAR, NEAR, ("x",)),
)


def ordered(value, old, new):
    if old == new:
        return value
    blocks = value.reshape((2,) * len(old) + (-1, value.shape[1]))
    axes = [old[::-1].index(flip) for flip in new[::-1]]
    return jnp.transpose(blocks, axes + [len(old), len(old) + 1]).reshape(value.shape)


def grown(value, flip):
    return jnp.concatenate([value, swap(value, *flip)], axis=0)


def added(a, b):
    return (a.astype(jnp.float32) + b.astype(jnp.float32)).astype(jnp.bfloat16)


def halved(value, flip):
    cut = value.shape[0] // 2
    return added(value[:cut], swap(value[cut:], *flip))


def ring_body(hidden_rows, routes, route_gain, gate_weight, up_weight, down_weight):
    n_lines = NZ * NY * NCORE
    block = hidden_rows[0]
    half, width = block.shape
    x, z, y, core = [lax.axis_index(name) for name in AXES]
    expert = (z * NY + y) * NCORE + core
    columns = gain_columns(
        lax.dynamic_slice_in_dim(routes[0], x * half, half, 0),
        lax.dynamic_slice_in_dim(route_gain[0], x * half, half, 0),
        n_lines,
    )

    def cut(edges):
        edges = [width * part // edges[-1] for part in edges]
        return [slice(start, stop) for start, stop in zip(edges, edges[1:])]

    spans, back_spans = cut(GATHER_EDGES), cut(SCATTER_EDGES)
    n_chunks = len(spans)
    dims = (((1,), (1,)), ((), ()))

    chunks = [block[:, span] for span in spans]
    one, two = (0, 1), (2, 3)
    in_far = [grown(chunks[c], FAR) for c in one]
    in_z = [grown(value, NEAR) for value in in_far]
    before_last = [grown(value, STAGES[c][2]) for c, value in zip(one, in_z)]
    flipped = [grown(after(chunks[c], *in_far), STAGES[c][0]) for c in two]
    at = GAIN_CHUNK - two[0]
    flipped[at] = jnp.concatenate([flipped[at], grown(after(columns, *in_far), STAGES[GAIN_CHUNK][0])], axis=1)
    flipped = [after(value, *in_z) for value in flipped]
    far = [jnp.concatenate([value, after(swap(value, *FAR), *before_last)], axis=0) for value in flipped]
    near = [grown(value, NEAR) for value in far]
    received = [swap(value, *STAGES[c][3]) for c, value in zip(one, before_last)]
    joined = lax.optimization_barrier(received + near)
    before_last += joined[2:]
    received = joined[:2] + [swap(before_last[c], *STAGES[c][3]) for c in two]

    halves = [{"gate": 0.0, "up": 0.0}, {"gate": 0.0, "up": 0.0}]
    for c in range(n_chunks):
        if c == 1:
            partial = halves[1]["up"]
        if c == 2:
            ties = [halves[0]["gate"], halves[0]["up"], halves[1]["gate"], partial]
            received[2:] = lax.optimization_barrier(received[2:] + ties)[:2]
        own = ordered(jnp.concatenate([before_last[c], received[c]], axis=0), STAGES[c], STAGES[0])
        for rows, sums in zip((own, swap(own, "core")), halves):
            if c == GAIN_CHUNK:
                lane = lax.broadcasted_iota(jnp.int32, (rows.shape[0], LANES), 1)
                gains = jnp.where(lax.rem(lane, n_lines) == expert, rows[:, -LANES:].astype(jnp.float32), 0.0)
                sums["gain"] = jnp.sum(gains, axis=1, keepdims=True)
                rows = rows[:, :-LANES]
            for name, weight in (("gate", gate_weight), ("up", up_weight)):
                sums[name] += lax.dot_general(rows, weight[0, :, spans[c]], dims, preferred_element_type=jnp.float32)

    def act(side, *before):
        gate, upper = after(halves[side]["gate"], *before), halves[side]["up"]
        value = (jax.nn.silu(gate) * upper * halves[side]["gain"]).astype(jnp.bfloat16)
        return lax.optimization_barrier(value)

    def down(value, c):
        return jnp.dot(value, down_weight[0, :, back_spans[c]], preferred_element_type=jnp.float32)

    away = act(1)
    to_core = {c: down(ordered(away, STAGES[0], STAGES[c]), c).astype(jnp.bfloat16) for c in two}
    here = act(0, *to_core.values())
    away = after(away, *to_core.values())
    to_core.update({c: down(ordered(away, STAGES[0], STAGES[c]), c).astype(jnp.bfloat16) for c in one})
    parts, kept, sent = {}, {}, {}
    for c in two + one:
        parts[c] = added(down(ordered(here, STAGES[0], STAGES[c]), c), swap(to_core[c], "core"))
        kept[c], goes = jnp.split(parts[c], 2, axis=0)
        sent[c] = swap(goes, *STAGES[c][3])
    first = {c: added(kept[c], sent[c]) for c in one}
    second = {c: halved(first[c], STAGES[c][2]) for c in one}
    outs = {}
    for c in two:
        value = added(kept[c], after(sent[c], *[parts[d] for d in one]))
        stays, goes = jnp.split(value, 2, axis=0)
        goes = swap(goes, *NEAR)
        value = added(stays, after(goes, *first.values()) if c == two[0] else goes)
        stays, goes = jnp.split(value, 2, axis=0)
        value = added(stays, after(swap(goes, *FAR), second[one[0]] if c == two[0] else first[one[0]]))
        outs[c] = (value, STAGES[c][0])
    for c in one:
        outs[c] = (halved(second[c], NEAR), FAR)
    for c, (value, flip) in outs.items():
        total = block[:, back_spans[c]].astype(jnp.float32) + value[:half].astype(jnp.float32)
        outs[c] = (total + swap(value[half:], *flip).astype(jnp.float32)).astype(jnp.bfloat16)
    return jnp.concatenate([outs[c] for c in range(n_chunks)], axis=1)[None]


def solution(mesh):
    small = dict(mesh.shape) == {"grp": NX, "attn": 1, "exp": NZ * NY * NCORE}
    if small:
        mesh = Mesh(mesh.devices.reshape(NX, NZ, NY, NCORE), AXES)
        exp, grp, attn, run = ("z", "y", "core"), "x", None, ring_body
    else:
        exp, grp, attn, run = "exp", "grp", "attn", body
    placed = (
        P(exp, grp, attn),
        P(exp, None, None),
        P(exp, None, None),
        P(exp, grp, attn),
        P(exp, grp, attn),
        P(exp, grp, attn),
    )
    return jax.shard_map(run, mesh=mesh, in_specs=placed, out_specs=P(exp, grp, attn), check_vma=False)
```
